32 devices in a mesh: cache: 4 (over z), head: 8 (over y, x, core).
Axes of the slice: x: 2, y: 2, z: 4, core: 2. Of those that a mesh axis runs over, the one named last changes fastest.
Arguments:
- delta_query: bfloat16 [16, 512, 2048], P('cache', None, 'head'), may hold values from -6 to 6
- delta_key: bfloat16 [16, 512, 2048], P('cache', None, 'head'), may hold values from -6 to 6
- delta_value: bfloat16 [16, 512, 4096], P('cache', None, 'head'), may hold values from -6 to 6
- delta_gate: bfloat16 [16, 512, 4096], P('cache', None, 'head'), may hold values from -6 to 6
- write_strength: float32 [16, 32, 512], P('cache', 'head'), may hold values from 0.1 to 0.95
- decay_log: float32 [16, 32, 512], P('cache', 'head'), may hold values from -1.5 to 0
- kept_state: float32 [16, 32, 128, 128], P('cache', 'head'), may hold values from -6 to 6
- kept_kv: bfloat16 [16, 1024, 2, 512], P('cache', 'head'), may hold values from -8 to 8
- fresh_kv: bfloat16 [16, 512, 2, 512], P('cache', 'head'), may hold values from -6 to 6
- attn_query: bfloat16 [16, 512, 4096], P('cache', None, 'head'), may hold values from -100 to 100
- attn_gate: bfloat16 [16, 512, 4096], P('cache', None, 'head'), may hold values from -6 to 6
- cached_len: int32 [16], replicated, may hold values from 2 to 1024, as said below
- slot_of_session: int32 [16], replicated, may hold values from 0 to 15, as said below
- delta_out_weight: bfloat16 [4096, 2048], P('head'), may hold values from -0.09375 to 0.09375
- attn_out_weight: bfloat16 [4096, 2048], P('head'), may hold values from -0.75 to 0.75
Outputs:
- delta_mixed: bfloat16 [8192, 2048], P(('cache', 'head'))
- attn_mixed: bfloat16 [8192, 2048], P(('cache', 'head'))
- final_state: float32 [16, 32, 128, 128], P('cache', 'head')
The draws below stay inside these ranges and needn't reach their ends.
Inputs may be any that keep to these rules, and one draw needn't show every extreme that they name: `slot_of_session`: a permutation of the slots; slot r lies on cache shard floor(r / 4); session s belongs to owner floor(s / 4), and the 4 sessions of one owner are kept on 4 different shards. `cached_len`: some session keeps exactly 1024 positions.
All inputs are finite; a program needn't handle non-finite values.
Results may differ from the reference program's by a relative error of at most 0.02.
Values may be sent and summed in bfloat16 or wider, within the bound.
A program may use at most 128 MiB of HBM per device.

```python
import math
import jax
import jax.numpy as jnp
from jax import lax

D = 2048
LQH = 16
LVH = 32
LK = 128
LV = 128
AH = 16
KVH = 2
HD = 256
NEW = 512
SESS_DEV = 4
LMAX = 1024
SESSIONS = 16
N_CACHE = 4
N_HEAD = 8


def draw_kept_kv(key, part):
    key = jax.random.fold_in(key, 7)
    cache = jax.random.truncated_normal(key, -6.0, 6.0, (SESSIONS, LMAX, 2, KVH * HD), jnp.float32)
    return cache.astype(jnp.bfloat16)


def draw_attn_query(key, part):
    key = jax.random.fold_in(key, 9)
    query_matrix = 1.5 * jax.random.truncated_normal(key, -6.0, 6.0, (SESSIONS, NEW, AH, HD), jnp.float32)
    return query_matrix.reshape(SESSIONS, NEW, AH * HD).astype(jnp.bfloat16)


def draw_cached_len(key, part):
    key = jax.random.fold_in(key, 3)
    first_key, second_key = jax.random.split(key)
    lengths = jax.random.randint(first_key, (SESSIONS,), 2, LMAX + 1)
    longest = jax.random.randint(second_key, (), 0, SESSIONS)
    return jnp.where(jnp.arange(SESSIONS) == longest, LMAX, lengths).astype(jnp.int32)


def draw_slot_of_session(key, part):
    key = jax.random.fold_in(key, 5)
    keys = jax.random.split(key, 4)
    owner_perm = jax.random.permutation(keys[0], N_CACHE)
    shard_perm = jax.random.permutation(keys[1], N_CACHE)
    shifts = jax.random.permutation(keys[2], N_CACHE)[:SESS_DEV]
    session_ids = jnp.arange(SESSIONS)
    owners = session_ids // SESS_DEV
    local = session_ids % SESS_DEV
    shard = shard_perm[(owner_perm[owners] + shifts[local]) % N_CACHE]
    within = jax.vmap(lambda sub: jax.random.permutation(sub, SESS_DEV))(jax.random.split(keys[3], N_CACHE))
    return (shard * SESS_DEV + within[shard, local]).astype(jnp.int32)


def draw_decay_log(key, part):
    key = jax.random.fold_in(key, 11)
    keys = jax.random.split(key, 5)
    shape_two = (SESSIONS, LVH)
    fast_cut = 5
    fast = jax.random.randint(keys[0], shape_two, 0, 10) < fast_cut
    fast_rate = jnp.exp(jax.random.uniform(keys[1], shape_two, jnp.float32, jnp.log(1.0 / 50.0), jnp.log(1.0 / 30.0)))
    slow_rate = jnp.exp(jax.random.uniform(keys[2], shape_two, jnp.float32, jnp.log(0.05 / NEW), jnp.log(0.5 / NEW)))
    forgetting_factor = jnp.where(fast, fast_rate, slow_rate)
    stored_entry_places = jax.random.randint(keys[3], shape_two + (2,), 0, NEW)
    objective_scores = jnp.log(jax.random.uniform(keys[4], shape_two + (2,), jnp.float32, 0.5, 0.8))
    sequence_offset = jnp.arange(NEW)
    prompt_segments = jnp.sum(jnp.where(sequence_offset[None, None, None, :] == stored_entry_places[..., None], objective_scores[..., None], 0.0), axis=2)
    return (prompt_segments - forgetting_factor[..., None]).astype(jnp.float32)


def levels(rng, extent, cuts, low, top_value):
    level, own = 1.0, jax.random.fold_in(rng, 6)
    for axis_at, blocks in cuts:
        draws = jnp.exp(jax.random.uniform(jax.random.fold_in(own, axis_at), (blocks,), jnp.float32, low / len(cuts), top_value / len(cuts)))
        level = level * jnp.repeat(draws, extent[axis_at] // blocks).reshape([-1 if axis == axis_at else 1 for axis in range(len(extent))])
    return level


def noise(stream_key, dims, deviation, reach, cuts=(), kind=jnp.bfloat16):
    drawn = deviation * jax.random.normal(stream_key, dims, jnp.float32)
    if cuts:
        drawn = drawn * levels(stream_key, dims, cuts, -0.22, 0.18)
    return jnp.clip(drawn, -reach, reach).astype(kind)


def setup_inputs(seed: int = 0) -> dict:
    streams_of = jax.random.split(jax.random.key(seed), 16)
    return {
        "delta_query": noise(streams_of[0], (SESSIONS, NEW, LQH * LK), 1.0, 6.0, ((0, 4), (2, 8))),
        "delta_key": noise(streams_of[1], (SESSIONS, NEW, LQH * LK), 1.0, 6.0, ((0, 4), (2, 8))),
        "delta_value": noise(streams_of[2], (SESSIONS, NEW, LVH * LV), 1.0, 6.0, ((0, 4), (2, 8))),
        "delta_gate": noise(streams_of[3], (SESSIONS, NEW, LVH * LV), 1.0, 6.0, ((0, 4), (2, 8))),
        "write_strength": jnp.clip(0.1 + 0.84999999 * jax.random.uniform(streams_of[4], (SESSIONS, LVH, NEW), jnp.float32) ** levels(streams_of[4], (SESSIONS, LVH, NEW), ((0, 4), (1, 8)), -0.2, 0.2), 0.1, 0.95),
        "decay_log": draw_decay_log(jax.random.fold_in(streams_of[15], 71), 0),
        "kept_state": noise(streams_of[6], (SESSIONS, LVH, LK, LV), 1.0, 6.0, ((0, 4), (1, 8)), jnp.float32),
        "kept_kv": draw_kept_kv(jax.random.fold_in(streams_of[15], 71), 0),
        "fresh_kv": noise(streams_of[8], (SESSIONS, NEW, 2, KVH * HD), 1.0, 6.0, ((0, 4), (1, 8))),
        "attn_query": draw_attn_query(jax.random.fold_in(streams_of[15], 71), 0),
        "attn_gate": noise(streams_of[10], (SESSIONS, NEW, AH * HD), 1.0, 6.0, ((0, 4), (2, 8))),
        "cached_len": draw_cached_len(jax.random.fold_in(streams_of[15], 71), 0),
        "slot_of_session": draw_slot_of_session(jax.random.fold_in(streams_of[15], 71), 0),
        "delta_out_weight": noise(streams_of[13], (LVH * LV, D), (LVH * LV) ** -0.5, 0.09375, ((0, 8),)),
        "attn_out_weight": noise(streams_of[14], (AH * HD, D), (HD // 4) ** -0.5, 0.75, ((0, 8),)),
    }


def unit_rows(matrix, epsilon):
    return matrix / jnp.sqrt(lax.optimization_barrier(jnp.sum(matrix * matrix, axis=-1, keepdims=True)) + epsilon)

def project_heads(heads, weight):
    group_cols = heads.shape[1] // N_HEAD
    aggregate_total = jnp.zeros((heads.shape[0], weight.shape[1]), jnp.float32)
    for group_id in range(N_HEAD):
        product_part = jnp.dot(heads[:, group_id * group_cols:(group_id + 1) * group_cols], weight[group_id * group_cols:(group_id + 1) * group_cols], preferred_element_type=jnp.float32)
        rounded = lax.optimization_barrier(product_part.astype(jnp.bfloat16))
        aggregate_total = aggregate_total + rounded.astype(jnp.float32)
    return aggregate_total.astype(jnp.bfloat16)

def delta_layer(delta_query, delta_key, delta_value, delta_gate, write_strength, decay_log, state_start):
    count = delta_query.shape[0]
    share_ratio = LVH // LQH
    query_matrix = unit_rows(delta_query.astype(jnp.float32).reshape(count, NEW, LQH, LK), 1e-06) * (1.0 / math.sqrt(LK))
    keyed = unit_rows(delta_key.astype(jnp.float32).reshape(count, NEW, LQH, LK), 1e-06)
    query_matrix = jnp.repeat(query_matrix, share_ratio, axis=2).transpose(1, 0, 2, 3)
    keyed = jnp.repeat(keyed, share_ratio, axis=2).transpose(1, 0, 2, 3)
    values = delta_value.astype(jnp.float32).reshape(count, NEW, LVH, LV).transpose(1, 0, 2, 3)
    strengths = write_strength.transpose(2, 0, 1)
    decays = decay_log.transpose(2, 0, 1)

    def advance(carried, pieces):
        q_now, k_now, v_now, b_now, g_now = pieces
        carried = jnp.exp(g_now)[:, :, None, None] * carried
        guess = jnp.einsum('shkv,shk->shv', carried, k_now, precision=lax.Precision.HIGHEST)
        update = b_now[:, :, None] * (v_now - guess)
        carried = carried + k_now[:, :, :, None] * update[:, :, None, :]
        emitted = jnp.einsum('shkv,shk->shv', carried, q_now, precision=lax.Precision.HIGHEST)
        return (carried, emitted)
    final_state, emitted = lax.scan(advance, state_start, (query_matrix, keyed, values, strengths, decays))
    emitted = emitted.transpose(1, 0, 2, 3)
    normed = emitted / jnp.sqrt(lax.optimization_barrier(jnp.mean(emitted * emitted, axis=-1, keepdims=True)) + 1e-06)
    gate_f = delta_gate.astype(jnp.float32).reshape(count, NEW, LVH, LV)
    heads = (normed * jax.nn.silu(gate_f)).astype(jnp.bfloat16).reshape(count * NEW, LVH * LV)
    return (heads, final_state)

def attend_session(pieces):
    query_rows, gate_rows, cache, fresh, length = pieces
    key_row_matrix = jnp.concatenate([cache[:, 0], fresh[:, 0]], axis=0).astype(jnp.float32).reshape(-1, KVH, HD)
    value_rows = jnp.concatenate([cache[:, 1], fresh[:, 1]], axis=0).astype(jnp.float32).reshape(-1, KVH, HD)
    head_kv = jnp.arange(AH) // (AH // KVH)
    key_row_matrix = key_row_matrix[:, head_kv]
    value_rows = value_rows[:, head_kv]
    query_matrix = query_rows.astype(jnp.float32).reshape(NEW, AH, HD)
    scores = jnp.einsum('thd,lhd->htl', query_matrix, key_row_matrix) * (1.0 / math.sqrt(HD))
    sequence_offset = jnp.arange(LMAX + NEW, dtype=jnp.int32)
    steps_new = jnp.arange(NEW, dtype=jnp.int32)
    usable = jnp.where(sequence_offset[None, :] < LMAX, sequence_offset[None, :] < length, sequence_offset[None, :] - LMAX <= steps_new[:, None])
    masked = jnp.where(usable[None], scores, -1e+30)
    peak_row = lax.optimization_barrier(jnp.max(masked, axis=-1, keepdims=True))
    weights = jnp.where(usable[None], jnp.exp(masked - peak_row), 0.0)
    total_w = lax.optimization_barrier(jnp.sum(weights, axis=-1))
    rounded = lax.optimization_barrier(weights.astype(jnp.bfloat16)).astype(jnp.float32)
    mixed = jnp.einsum('htl,lhd->thd', rounded, value_rows) / total_w.T[:, :, None]
    gated = jax.nn.sigmoid(gate_rows.astype(jnp.float32).reshape(NEW, AH, HD)) * mixed
    return gated.reshape(NEW, AH * HD).astype(jnp.bfloat16)

def reference(delta_query, delta_key, delta_value, delta_gate, write_strength, decay_log, kept_state, kept_kv, fresh_kv, attn_query, attn_gate, cached_len, slot_of_session, delta_out_weight, attn_out_weight):
    slots = slot_of_session.astype(jnp.int32)
    state_start = jnp.take(kept_state, slots, axis=0)
    cache_start = jnp.take(kept_kv, slots, axis=0)
    delta_heads, final_state = delta_layer(delta_query, delta_key, delta_value, delta_gate, write_strength, decay_log, state_start)
    delta_mixed = project_heads(delta_heads, delta_out_weight)
    attn_heads = lax.map(attend_session, (attn_query, attn_gate, cache_start, fresh_kv, cached_len))
    attn_heads = attn_heads.reshape(-1, AH * HD)
    attn_mixed = project_heads(attn_heads, attn_out_weight)
    return (delta_mixed, attn_mixed, final_state)
```

```python
import functools
import math

import jax
import jax.numpy as jnp
from jax import lax
from jax.experimental import pallas as pl
from jax.experimental.pallas import tpu as pltpu
from jax.sharding import PartitionSpec as P

LK = 128
LV = 128
AH = 16
KVH = 2
HD = 256
BLOCK = 128
PAIR = 2
CHUNKS = 2

big_negative = -1e30
f32 = jnp.float32
bf16 = jnp.bfloat16


def mm(a, b, dims=((1,), (0,))):
    return lax.dot_general(a, b, (dims, ((), ())), preferred_element_type=f32)


def delta_kernel(source, q_ref, k_ref, v_ref, gate_ref, row_ref, col_ref, start_ref, heads_ref, state_ref):
    pair = pl.program_id(0)
    sessions, _, q_cols = q_ref.shape
    key_heads = q_cols // LK
    value_heads = v_ref.shape[2] // LV
    ratio = value_heads // key_heads

    @pl.when(pl.program_id(1) == 0)
    def _():
        for s in range(sessions):
            state_ref[s] = start_ref[source[pair * sessions + s]].astype(f32)

    rows = lax.broadcasted_iota(jnp.int32, (BLOCK, BLOCK), 0)
    cols = lax.broadcasted_iota(jnp.int32, (BLOCK, BLOCK), 1)
    inclusive = rows >= cols
    differ = jnp.where(rows > cols, rows ^ cols, 0)
    eye = jnp.where(rows == cols, 1.0, 0.0).astype(f32)

    work = []
    for s in range(sessions):
        for a in range(key_heads):
            span = slice(a * LK, (a + 1) * LK)
            q = q_ref[s, :, span].astype(f32)
            k = k_ref[s, :, span].astype(f32)
            q = q * (lax.rsqrt(jnp.sum(q * q, axis=-1, keepdims=True) + 1e-06) * (1.0 / math.sqrt(LK)))
            k = k * lax.rsqrt(jnp.sum(k * k, axis=-1, keepdims=True) + 1e-06)
            qb, kb = q.astype(bf16), k.astype(bf16)
            key_key = mm(kb, kb, ((1,), (1,)))
            query_key = mm(qb, kb, ((1,), (1,)))
            for j in range(a * ratio, (a + 1) * ratio):
                run_row = row_ref[s, j : j + 1, :]
                run_col = col_ref[s, :, j : j + 1]
                strength = col_ref[s, :, value_heads + j : value_heads + j + 1]
                fall = jnp.where(inclusive, jnp.exp(jnp.minimum(run_col - run_row, 0.0)), 0.0)
                lower = strength * fall * key_key
                mixed = (fall * query_key).astype(bf16)
                growth = jnp.exp(run_col)
                v = v_ref[s, :, j * LV : (j + 1) * LV].astype(f32)
                right = jnp.concatenate([(strength * growth) * k, strength * v], axis=1).astype(bf16)
                last = run_row[:, BLOCK - 1 : BLOCK]
                tail = (jnp.exp(last - run_col) * k).astype(bf16)
                work.append((s, j, lower, mixed, (growth * q).astype(bf16), right, tail, jnp.exp(last)))

    inverses = [eye - jnp.where(differ == 1, item[2], 0.0) for item in work]
    for level in range(1, BLOCK.bit_length() - 1):
        mask = (differ >> level) == 1
        small = [t.astype(bf16) for t in inverses]
        first = [
            mm(jnp.where(mask, item[2], 0.0).astype(bf16), t).astype(bf16) for item, t in zip(work, small)
        ]
        inverses = [t - mm(b, x) for t, b, x in zip(inverses, small, first)]

    solved = [mm(t.astype(bf16), item[5]) for t, item in zip(inverses, work)]
    for item, x in zip(work, solved):
        s, j, _, mixed, q_grown, _, tail, fade = item
        state = state_ref[s, j]
        seen = mm(jnp.concatenate([x[:, :LK].astype(bf16), q_grown], axis=0), state.astype(bf16))
        update = (x[:, LK:] - seen[:BLOCK]).astype(bf16)
        state_ref[s, j] = fade * state + mm(tail, update, ((0,), (0,)))
        emitted = seen[BLOCK:] + mm(mixed, update)
        scale = lax.rsqrt(jnp.mean(emitted * emitted, axis=-1, keepdims=True) + 1e-06)
        gate = gate_ref[s, :, j * LV : (j + 1) * LV].astype(f32)
        heads_ref[s, :, j * LV : (j + 1) * LV] = (emitted * scale * (gate / (1.0 + jnp.exp(-gate)))).astype(bf16)


def delta_layer(q, k, v, gate, strength, decay, start, source):
    count, fresh_len, value_cols = v.shape
    value_heads = value_cols // LV
    running = jnp.cumsum(decay.reshape(count, value_heads, fresh_len // BLOCK, BLOCK), axis=-1)
    running = running.reshape(count, value_heads, fresh_len)
    columns = jnp.concatenate([running, strength], axis=1).transpose(0, 2, 1)

    def rows(width):
        return pl.BlockSpec((PAIR, BLOCK, width), lambda s, c, _: (s, c, 0))

    return pl.pallas_call(
        delta_kernel,
        grid_spec=pltpu.PrefetchScalarGridSpec(
            num_scalar_prefetch=1,
            grid=(count // PAIR, fresh_len // BLOCK),
            in_specs=[
                rows(q.shape[2]),
                rows(k.shape[2]),
                rows(value_cols),
                rows(value_cols),
                pl.BlockSpec((PAIR, value_heads, BLOCK), lambda s, c, _: (s, 0, c)),
                rows(2 * value_heads),
                pl.BlockSpec(start.shape, lambda s, c, _: (0, 0, 0, 0)),
            ],
            out_specs=[
                rows(value_cols),
                pl.BlockSpec((PAIR, value_heads, LK, LV), lambda s, c, _: (s, 0, 0, 0)),
            ],
        ),
        out_shape=[
            jax.ShapeDtypeStruct((count, fresh_len, value_cols), bf16),
            jax.ShapeDtypeStruct((count, value_heads, LK, LV), f32),
        ],
        compiler_params=pltpu.CompilerParams(vmem_limit_bytes=40 * 2**20),
        cost_estimate=pl.CostEstimate(flops=4 * 10**10, bytes_accessed=12 * 10**6, transcendentals=0),
        name="delta_layer",
    )(source, q, k, v, gate, running, columns, start)


def attend_kernel(chunk, block_rows, devices, scalars, lengths, q_ref, gate_ref, near_ref, far_ref, fresh_ref, out_ref):
    s = pl.program_id(0)
    me = scalars[1]
    length = lengths[s]
    _, blocks, part, width = q_ref.shape
    rows = blocks * part
    heads = width // HD
    slots, _, _, kept_rows, _ = near_ref.shape
    kept = slots * kept_rows
    bits = devices.bit_length() - 1

    def penalty(far):
        lane = lax.broadcasted_iota(jnp.int32, (1, kept), 1)
        slot = lane // kept_rows + far * slots
        code = jnp.zeros_like(slot)
        for i in range(bits):
            code = code + ((slot >> i) & 1) * (1 << (bits - 1 - i))
        place = (code ^ me) * kept_rows + lane % kept_rows
        return jnp.where(place < length, 0.0, big_negative).astype(f32)

    fresh = fresh_ref.shape[0] * fresh_ref.shape[3]
    row = lax.broadcasted_iota(jnp.int32, (rows, fresh), 0)
    now = (row // part) * block_rows + chunk * part + row % part
    causal = lax.broadcasted_iota(jnp.int32, (rows, fresh), 1) <= now
    near_off, far_off = penalty(0), penalty(1)

    keys = [
        near_ref[:, 0, 0].reshape(kept, HD),
        far_ref[:, 0, 0].reshape(kept, HD),
        fresh_ref[:, 0, 0].reshape(fresh, HD),
    ]
    values = [
        near_ref[:, 0, 1].reshape(kept, HD),
        far_ref[:, 0, 1].reshape(kept, HD),
        fresh_ref[:, 1, 0].reshape(fresh, HD),
    ]
    for h in range(heads):
        q = q_ref[0, :, :, h * HD : (h + 1) * HD].reshape(rows, HD)
        near = mm(q, keys[0], ((1,), (1,))) + near_off
        far = mm(q, keys[1], ((1,), (1,))) + far_off
        new = jnp.where(causal, mm(q, keys[2], ((1,), (1,))), big_negative)
        peak = jnp.max(jnp.maximum(jnp.maximum(near, far), new) if kept == fresh else new, axis=-1, keepdims=True)
        if kept != fresh:
            peak = jnp.maximum(peak, jnp.max(jnp.maximum(near, far), axis=-1, keepdims=True))
        weights = [jnp.exp((x - peak) * (1.0 / math.sqrt(HD))) for x in (near, far, new)]
        total = sum(jnp.sum(w, axis=-1, keepdims=True) for w in weights)
        mixed = sum(mm(w.astype(bf16), v) for w, v in zip(weights, values))
        gate = gate_ref[0, :, :, h * HD : (h + 1) * HD].reshape(rows, HD).astype(f32)
        gated = mixed / (total * (1.0 + jnp.exp(-gate)))
        out_ref[0, :, :, h * HD : (h + 1) * HD] = gated.astype(bf16).reshape(blocks, part, HD)


def attend(chunk, block_rows, devices, q, gate, near, far, fresh, scalars, lengths, source):
    count, blocks, _, width = q.shape
    part = block_rows // CHUNKS
    scalars = jnp.concatenate([scalars, source])
    slots, _, _, kept_rows, _ = near.shape
    rows = pl.BlockSpec((1, blocks, part, width), lambda s, m, n: (s, 0, chunk, 0))
    kept = pl.BlockSpec((slots, 1, 2, kept_rows, HD), lambda s, m, n: (0, m[2 + s], 0, 0, 0))
    return pl.pallas_call(
        functools.partial(attend_kernel, chunk, block_rows, devices),
        grid_spec=pltpu.PrefetchScalarGridSpec(
            num_scalar_prefetch=2,
            grid=(count,),
            in_specs=[
                rows,
                rows,
                kept,
                kept,
                pl.BlockSpec(
                    (fresh.shape[0], 2, 1, fresh.shape[3], HD), lambda s, m, n: (0, 0, s, 0, m[0])
                ),
            ],
            out_specs=pl.BlockSpec((1, blocks, part, width), lambda s, m, n: (s, 0, 0, 0)),
        ),
        out_shape=jax.ShapeDtypeStruct((count, blocks, part, width), bf16),
        compiler_params=pltpu.CompilerParams(vmem_limit_bytes=48 * 2**20),
        cost_estimate=pl.CostEstimate(flops=10**10, bytes_accessed=8 * 10**6, transcendentals=0),
        name="attend",
    )(scalars, lengths, q, gate, near, far, fresh)


def swap(x, devices, bit):
    return lax.ppermute(x, "head", [(h, h ^ bit) for h in range(devices)])


def halves(x, me, bit, lowest):
    split = x.reshape(x.shape[0] // (2 * lowest), 2, lowest, *x.shape[1:])
    mine = (me // bit) % 2

    def pick(which):
        got = lax.dynamic_index_in_dim(split, which, 1, keepdims=False)
        return got.reshape(x.shape[0] // 2, *x.shape[1:])

    return pick(mine), pick(1 - mine)


def add(a, b):
    return (a.astype(f32) + b.astype(f32)).astype(bf16)


def project(heads, weight, devices, me):
    bits = devices.bit_length() - 1
    kept, sent = halves(heads, me, 1, 1)

    def product(x):
        out = jnp.dot(x.reshape(-1, x.shape[2]), weight, preferred_element_type=f32)
        return out.astype(bf16).reshape(x.shape[0], x.shape[1], -1)

    arrived = swap(product(sent), devices, 1)
    total = add(product(kept), arrived)
    wide = total.shape[2] // 2
    done = []
    for side, order in enumerate((range(1, bits), range(bits - 1, 0, -1))):
        part = total[:, :, side * wide : (side + 1) * wide]
        left = list(range(1, bits))
        for bit in order:
            mine, other = halves(part, me, 1 << bit, 1 << left.index(bit))
            left.remove(bit)
            part = add(mine, swap(other, devices, 1 << bit))
        done.append(part[0])
    return jnp.concatenate(done, axis=1)


def on_device(
    delta_query,
    delta_key,
    delta_value,
    delta_gate,
    write_strength,
    decay_log,
    kept_state,
    kept_kv,
    fresh_kv,
    attn_query,
    attn_gate,
    cached_len,
    slot_of_session,
    delta_out_weight,
    attn_out_weight,
):
    count, fresh_len, query_cols = attn_query.shape
    owners = lax.axis_size("cache")
    devices = lax.axis_size("head")
    owner_id = lax.axis_index("cache")
    me = lax.axis_index("head")
    session_ids = jnp.arange(slot_of_session.shape[0], dtype=jnp.int32)
    on_mine = slot_of_session // count == owner_id
    owner_of = session_ids // count
    wanted = on_mine[None, :] & (owner_of[None, :] == jnp.arange(owners, dtype=jnp.int32)[:, None])
    picked_slot = jnp.sum(jnp.where(wanted, slot_of_session[None, :] - owner_id * count, 0), axis=1)
    my_slots = lax.dynamic_slice_in_dim(slot_of_session, owner_id * count, count)
    source = my_slots // count
    lengths = lax.dynamic_slice_in_dim(cached_len, owner_id * count, count)

    def exchange(x):
        return lax.all_to_all(x, "cache", split_axis=0, concat_axis=0, tiled=True)

    def pick(x):
        return jnp.concatenate([lax.dynamic_slice_in_dim(x, picked_slot[o], 1, 0) for o in range(owners)], axis=0)

    start = exchange(pick(kept_state).astype(bf16))
    landed = exchange(pick(kept_kv.transpose(0, 2, 1, 3)))

    heads_dev = query_cols // HD
    kv_head = me * heads_dev // (AH // KVH)
    fresh_all = lax.all_gather(fresh_kv.transpose(2, 0, 1, 3), "head", axis=0, tiled=False)

    own = lax.dynamic_slice_in_dim(landed, kv_head * HD, HD, 3)
    other = lax.dynamic_slice_in_dim(landed, (1 - kv_head) * HD, HD, 3)
    half = devices // 2
    near = jnp.stack([own, swap(other, devices, half)])
    bit = half // 2
    while bit > 1:
        near = jnp.concatenate([near, swap(near, devices, bit)], axis=0)
        bit //= 2
    far = swap(near, devices, 1)

    delta_heads, final_state = delta_layer(
        delta_query, delta_key, delta_value, delta_gate, write_strength, decay_log, start, source
    )
    block_rows = count * fresh_len // devices
    delta_mixed = project(delta_heads.reshape(devices, block_rows, -1), delta_out_weight, devices, me)

    scalars = jnp.stack([kv_head, me]).astype(jnp.int32)
    q4 = attn_query.reshape(count, fresh_len // block_rows, block_rows, query_cols)
    gate4 = attn_gate.reshape(q4.shape)
    done = []
    for chunk in range(CHUNKS):
        heads = attend(
            chunk, block_rows, devices, q4, gate4, near, far, fresh_all, scalars, lengths, source
        )
        heads = heads.reshape(devices, block_rows // CHUNKS, query_cols)
        done.append(project(heads, attn_out_weight, devices, me))
    return (delta_mixed, jnp.concatenate(done, axis=0), final_state)


def solution(mesh):
    in_specs = (
        P("cache", None, "head"),
        P("cache", None, "head"),
        P("cache", None, "head"),
        P("cache", None, "head"),
        P("cache", "head", None),
        P("cache", "head", None),
        P("cache", "head", None, None),
        P("cache", "head", None, None),
        P("cache", "head", None, None),
        P("cache", None, "head"),
        P("cache", None, "head"),
        P(),
        P(),
        P("head", None),
        P("head", None),
    )
    out_specs = (
        P(("cache", "head"), None),
        P(("cache", "head"), None),
        P("cache", "head", None, None),
    )
    return jax.shard_map(
        on_device, mesh=mesh, in_specs=in_specs, out_specs=out_specs, check_vma=False
    )
```

```python
import functools
import math

import jax
import jax.numpy as jnp
from jax import lax
from jax.experimental import pallas as pl
from jax.experimental.pallas import tpu as pltpu
from jax.sharding import PartitionSpec as P

LK = 128
LV = 128
AH = 16
KVH = 2
HD = 256
BLOCK = 128
PAIR = 2
PARTS = 2
CHUNKS = 2

big_negative = -1e30
f32 = jnp.float32
bf16 = jnp.bfloat16


def mm(a, b, dims=((1,), (0,))):
    return lax.dot_general(a, b, (dims, ((), ())), preferred_element_type=f32)


def delta_kernel(deps, source, q_ref, k_ref, v_ref, gate_ref, row_ref, col_ref, start_ref, *refs):
    heads_ref, state_ref = refs[deps:]
    sessions, _, q_cols = q_ref.shape
    key_heads = q_cols // LK
    value_heads = v_ref.shape[2] // LV
    ratio = value_heads // key_heads

    @pl.when(pl.program_id(0) == 0)
    def _():
        for s in range(sessions):
            state_ref[s] = start_ref[source[s]].astype(f32)

    rows = lax.broadcasted_iota(jnp.int32, (BLOCK, BLOCK), 0)
    cols = lax.broadcasted_iota(jnp.int32, (BLOCK, BLOCK), 1)
    inclusive = rows >= cols
    differ = jnp.where(rows > cols, rows ^ cols, 0)
    eye = jnp.where(rows == cols, 1.0, 0.0).astype(f32)

    work = []
    for s in range(sessions):
        for a in range(key_heads):
            span = slice(a * LK, (a + 1) * LK)
            q = q_ref[s, :, span].astype(f32)
            k = k_ref[s, :, span].astype(f32)
            q = q * (lax.rsqrt(jnp.sum(q * q, axis=-1, keepdims=True) + 1e-06) * (1.0 / math.sqrt(LK)))
            k = k * lax.rsqrt(jnp.sum(k * k, axis=-1, keepdims=True) + 1e-06)
            qb, kb = q.astype(bf16), k.astype(bf16)
            key_key = mm(kb, kb, ((1,), (1,)))
            query_key = mm(qb, kb, ((1,), (1,)))
            for j in range(a * ratio, (a + 1) * ratio):
                run_row = row_ref[s, j : j + 1, :]
                run_col = col_ref[s, :, j : j + 1]
                strength = col_ref[s, :, value_heads + j : value_heads + j + 1]
                fall = jnp.where(inclusive, jnp.exp(jnp.minimum(run_col - run_row, 0.0)), 0.0)
                lower = strength * fall * key_key
                mixed = (fall * query_key).astype(bf16)
                growth = jnp.exp(run_col)
                v = v_ref[s, :, j * LV : (j + 1) * LV].astype(f32)
                right = jnp.concatenate([(strength * growth) * k, strength * v], axis=1).astype(bf16)
                last = run_row[:, BLOCK - 1 : BLOCK]
                tail = (jnp.exp(last - run_col) * k).astype(bf16)
                work.append((s, j, lower, mixed, (growth * q).astype(bf16), right, tail, jnp.exp(last)))

    inverses = [eye - jnp.where(differ == 1, item[2], 0.0) for item in work]
    for level in range(1, BLOCK.bit_length() - 1):
        mask = (differ >> level) == 1
        small = [t.astype(bf16) for t in inverses]
        first = [
            mm(jnp.where(mask, item[2], 0.0).astype(bf16), t).astype(bf16) for item, t in zip(work, small)
        ]
        inverses = [t - mm(b, x) for t, b, x in zip(inverses, small, first)]

    solved = [mm(t.astype(bf16), item[5]) for t, item in zip(inverses, work)]
    for item, x in zip(work, solved):
        s, j, _, mixed, q_grown, _, tail, fade = item
        state = state_ref[s, j]
        seen = mm(jnp.concatenate([x[:, :LK].astype(bf16), q_grown], axis=0), state.astype(bf16))
        update = (x[:, LK:] - seen[:BLOCK]).astype(bf16)
        state_ref[s, j] = fade * state + mm(tail, update, ((0,), (0,)))
        emitted = seen[BLOCK:] + mm(mixed, update)
        scale = lax.rsqrt(jnp.mean(emitted * emitted, axis=-1, keepdims=True) + 1e-06)
        gate = gate_ref[s, :, j * LV : (j + 1) * LV].astype(f32)
        heads_ref[s, :, j * LV : (j + 1) * LV] = (emitted * scale * (gate / (1.0 + jnp.exp(-gate)))).astype(bf16)


def block_rates(strength, decay):
    count, value_heads, fresh_len = decay.shape
    upto = jnp.triu(jnp.ones((BLOCK, BLOCK), f32))
    running = jnp.matmul(decay.reshape(-1, BLOCK), upto, precision=lax.Precision.HIGHEST)
    running = running.reshape(count, value_heads, fresh_len)
    return running, jnp.concatenate([running, strength], axis=1).transpose(0, 2, 1)


def delta_part(q, k, v, gate, running, columns, start, places, heads, pair, part, deps):
    count, fresh_len, value_cols = v.shape
    value_heads = value_cols // LV
    steps = fresh_len // BLOCK // PARTS
    unread = ([] if heads is None else [heads]) + list(deps)

    def rows(width):
        return pl.BlockSpec((PAIR, BLOCK, width), lambda c, _: (pair, part * steps + c, 0))

    return pl.pallas_call(
        functools.partial(delta_kernel, len(unread)),
        grid_spec=pltpu.PrefetchScalarGridSpec(
            num_scalar_prefetch=1,
            grid=(steps,),
            in_specs=[
                rows(q.shape[2]),
                rows(k.shape[2]),
                rows(value_cols),
                rows(value_cols),
                pl.BlockSpec((PAIR, value_heads, BLOCK), lambda c, _: (pair, 0, part * steps + c)),
                rows(2 * value_heads),
                pl.BlockSpec(start.shape, lambda c, _: (0, 0, 0, 0)),
            ]
            + [pl.BlockSpec(memory_space=pl.ANY)] * len(unread),
            out_specs=[
                rows(value_cols),
                pl.BlockSpec((PAIR, value_heads, LK, LV), lambda c, _: (0, 0, 0, 0)),
            ],
        ),
        out_shape=[
            jax.ShapeDtypeStruct((count, fresh_len, value_cols), bf16),
            jax.ShapeDtypeStruct((PAIR, value_heads, LK, LV), f32),
        ],
        input_output_aliases={} if heads is None else {8: 0},
        compiler_params=pltpu.CompilerParams(vmem_limit_bytes=32 * 2**20),
        cost_estimate=pl.CostEstimate(flops=10**10, bytes_accessed=3 * 10**6, transcendentals=0),
        name="delta_part",
    )(places, q, k, v, gate, running, columns, start, *unread)


def attend_kernel(chunk, block_rows, devices, scalars, lengths, q_ref, gate_ref, near_ref, far_ref, fresh_ref, *refs):
    out_ref = refs[-1]
    s = pl.program_id(0)
    me = scalars[1]
    length = lengths[s]
    _, blocks, part, width = q_ref.shape
    rows = blocks * part
    heads = width // HD
    slots, _, _, kept_rows, _ = near_ref.shape
    kept = slots * kept_rows
    bits = devices.bit_length() - 1

    def penalty(far):
        lane = lax.broadcasted_iota(jnp.int32, (1, kept), 1)
        slot = lane // kept_rows + far * slots
        code = jnp.zeros_like(slot)
        for i in range(bits):
            code = code + ((slot >> i) & 1) * (1 << (bits - 1 - i))
        place = (code ^ me) * kept_rows + lane % kept_rows
        return jnp.where(place < length, 0.0, big_negative).astype(f32)

    fresh = fresh_ref.shape[0] * fresh_ref.shape[3]
    row = lax.broadcasted_iota(jnp.int32, (rows, fresh), 0)
    now = (row // part) * block_rows + chunk * part + row % part
    causal = lax.broadcasted_iota(jnp.int32, (rows, fresh), 1) <= now
    near_off, far_off = penalty(0), penalty(1)

    keys = [
        near_ref[:, 0, 0].reshape(kept, HD),
        far_ref[:, 0, 0].reshape(kept, HD),
        fresh_ref[:, 0, 0].reshape(fresh, HD),
    ]
    values = [
        near_ref[:, 0, 1].reshape(kept, HD),
        far_ref[:, 0, 1].reshape(kept, HD),
        fresh_ref[:, 1, 0].reshape(fresh, HD),
    ]
    for h in range(heads):
        q = q_ref[0, :, :, h * HD : (h + 1) * HD].reshape(rows, HD)
        near = mm(q, keys[0], ((1,), (1,))) + near_off
        far = mm(q, keys[1], ((1,), (1,))) + far_off
        new = jnp.where(causal, mm(q, keys[2], ((1,), (1,))), big_negative)
        peak = jnp.max(jnp.maximum(jnp.maximum(near, far), new) if kept == fresh else new, axis=-1, keepdims=True)
        if kept != fresh:
            peak = jnp.maximum(peak, jnp.max(jnp.maximum(near, far), axis=-1, keepdims=True))
        weights = [jnp.exp((x - peak) * (1.0 / math.sqrt(HD))) for x in (near, far, new)]
        total = sum(jnp.sum(w, axis=-1, keepdims=True) for w in weights)
        mixed = sum(mm(w.astype(bf16), v) for w, v in zip(weights, values))
        gate = gate_ref[0, :, :, h * HD : (h + 1) * HD].reshape(rows, HD).astype(f32)
        gated = mixed / (total * (1.0 + jnp.exp(-gate)))
        out_ref[0, :, :, h * HD : (h + 1) * HD] = gated.astype(bf16).reshape(blocks, part, HD)


def attend(chunk, block_rows, devices, q, gate, near, far, fresh, scalars, lengths, places, deps):
    count, blocks, _, width = q.shape
    part = block_rows // CHUNKS
    scalars = jnp.concatenate([scalars, places])
    slots, _, _, kept_rows, _ = near.shape
    rows = pl.BlockSpec((1, blocks, part, width), lambda s, m, n: (s, 0, chunk, 0))
    kept = pl.BlockSpec((slots, 1, 2, kept_rows, HD), lambda s, m, n: (0, m[2 + s], 0, 0, 0))
    return pl.pallas_call(
        functools.partial(attend_kernel, chunk, block_rows, devices),
        grid_spec=pltpu.PrefetchScalarGridSpec(
            num_scalar_prefetch=2,
            grid=(count,),
            in_specs=[
                rows,
                rows,
                kept,
                kept,
                pl.BlockSpec(
                    (fresh.shape[0], 2, 1, fresh.shape[3], HD), lambda s, m, n: (0, 0, s, 0, m[0])
                ),
            ]
            + [pl.BlockSpec(memory_space=pl.ANY)] * len(deps),
            out_specs=pl.BlockSpec((1, blocks, part, width), lambda s, m, n: (s, 0, 0, 0)),
        ),
        out_shape=jax.ShapeDtypeStruct((count, blocks, part, width), bf16),
        compiler_params=pltpu.CompilerParams(vmem_limit_bytes=48 * 2**20),
        cost_estimate=pl.CostEstimate(flops=10**10, bytes_accessed=8 * 10**6, transcendentals=0),
        name="attend",
    )(scalars, lengths, q, gate, near, far, fresh, *deps)


def swap(x, devices, bit, axis="head"):
    return lax.ppermute(x, axis, [(h, h ^ bit) for h in range(devices)])


def halves(x, me, bit, lowest):
    split = x.reshape(x.shape[0] // (2 * lowest), 2, lowest, *x.shape[1:])
    mine = (me // bit) % 2

    def pick(which):
        got = lax.dynamic_index_in_dim(split, which, 1, keepdims=False)
        return got.reshape(x.shape[0] // 2, *x.shape[1:])

    return pick(mine), pick(1 - mine)


def add(a, b):
    return (a.astype(f32) + b.astype(f32)).astype(bf16)


def product(x, weight):
    out = jnp.dot(x.reshape(-1, x.shape[2]), weight, preferred_element_type=f32)
    return out.astype(bf16).reshape(x.shape[0], x.shape[1], -1)


def project_first(heads, weight, devices, me):
    kept, sent = halves(heads, me, 1, 1)
    return add(product(kept, weight), swap(product(sent, weight), devices, 1))


def project_next(parts, devices, me):
    bits = devices.bit_length() - 1
    orders = (list(range(1, bits)), list(range(bits - 1, 0, -1)))
    done = []
    for part, order in zip(parts, orders):
        left = part.shape[0].bit_length() - 1
        bit = order[bits - 1 - left]
        below = sum(1 for b in order[bits - 1 - left :] if b < bit)
        mine, other = halves(part, me, 1 << bit, 1 << below)
        done.append(add(mine, swap(other, devices, 1 << bit)))
    return done


def column_halves(total):
    wide = total.shape[2] // 2
    return [total[:, :, :wide], total[:, :, wide:]]


def project_rest(parts, devices, me):
    while parts[0].shape[0] > 1:
        parts = project_next(parts, devices, me)
    return jnp.concatenate([p[0] for p in parts], axis=1)


def on_device(
    delta_query,
    delta_key,
    delta_value,
    delta_gate,
    write_strength,
    decay_log,
    kept_state,
    kept_kv,
    fresh_kv,
    attn_query,
    attn_gate,
    cached_len,
    slot_of_session,
    delta_out_weight,
    attn_out_weight,
):
    count, fresh_len, query_cols = attn_query.shape
    owners = lax.axis_size("cache")
    devices = lax.axis_size("head")
    owner_id = lax.axis_index("cache")
    me = lax.axis_index("head")
    session_ids = jnp.arange(slot_of_session.shape[0], dtype=jnp.int32)
    on_mine = slot_of_session // count == owner_id
    owner_of = session_ids // count
    wanted = on_mine[None, :] & (owner_of[None, :] == jnp.arange(owners, dtype=jnp.int32)[:, None])
    picked_slot = jnp.sum(jnp.where(wanted, slot_of_session[None, :] - owner_id * count, 0), axis=1)
    my_slots = lax.dynamic_slice_in_dim(slot_of_session, owner_id * count, count)
    source = my_slots // count
    lengths = lax.dynamic_slice_in_dim(cached_len, owner_id * count, count)

    places = source ^ owner_id

    def send_on(x, distance):
        block = lax.dynamic_slice_in_dim(x, picked_slot[owner_id ^ distance], 1, 0)
        return swap(block, owners, distance, "cache") if distance else block

    state_bf16 = kept_state.astype(bf16)
    start = jnp.concatenate([send_on(state_bf16, r) for r in range(owners)], axis=0)

    heads_dev = query_cols // HD
    kv_head = me * heads_dev // (AH // KVH)
    fresh_all = lax.all_gather(fresh_kv.transpose(2, 0, 1, 3), "head", axis=0, tiled=False)

    half = devices // 2
    own = lax.dynamic_slice_in_dim(kept_kv, kv_head * HD, HD, 3).transpose(0, 2, 1, 3)
    other = lax.dynamic_slice_in_dim(kept_kv, (1 - kv_head) * HD, HD, 3).transpose(0, 2, 1, 3)
    both = jnp.stack([own, swap(other, devices, half)], axis=1)
    blocks = [send_on(both, r) for r in range(owners)]

    calls = count // PAIR * PARTS
    bit = half // 2
    crossed = [swap(block, devices, bit) for block in blocks]
    needed = [[] for _ in range(calls - 1)]
    for r in range(1, owners):
        arrival = min((r - 1) * (calls - 1) // (owners - 1), calls - 2)
        needed[arrival].append(blocks[r])
        if arrival + 1 < calls - 1:
            needed[arrival + 1].append(crossed[r])
    needed[min(1, calls - 2)].append(crossed[0])
    needed[-1].append(fresh_all)

    running, columns = block_rates(write_strength, decay_log)
    heads, states, call = None, [], 0
    for pair in range(count // PAIR):
        begin, index = start, lax.slice_in_dim(places, pair * PAIR, (pair + 1) * PAIR)
        for part in range(PARTS):
            deps = needed[call - 1] if call else []
            heads, begin = delta_part(
                delta_query,
                delta_key,
                delta_value,
                delta_gate,
                running,
                columns,
                begin,
                index,
                heads,
                pair,
                part,
                deps,
            )
            index = jnp.arange(PAIR, dtype=jnp.int32)
            call += 1
        states.append(begin)
    final_state = jnp.concatenate(states, axis=0)

    near = [jnp.stack([x[0] for x in side], axis=1) for side in (blocks, crossed)]
    near = jnp.concatenate(near, axis=0)
    bit //= 2
    while bit > 1:
        near = jnp.concatenate([near, swap(near, devices, bit)], axis=0)
        bit //= 2
    far = swap(near, devices, 1)

    block_rows = count * fresh_len // devices
    total = project_first(heads.reshape(devices, block_rows, -1), delta_out_weight, devices, me)
    scalars = jnp.stack([kv_head, me]).astype(jnp.int32)
    q4 = attn_query.reshape(count, fresh_len // block_rows, block_rows, query_cols)
    gate4 = attn_gate.reshape(q4.shape)
    parts = column_halves(total)
    deps = [total]
    done = []
    for chunk in range(CHUNKS):
        mixed = attend(
            chunk, block_rows, devices, q4, gate4, near, far, fresh_all, scalars, lengths, places, deps
        )
        mixed = mixed.reshape(devices, block_rows // CHUNKS, query_cols)
        total = project_first(mixed, attn_out_weight, devices, me)
        if parts[0].shape[0] > 1:
            parts = project_next(parts, devices, me)
        deps = [total, *parts]
        done.append(total)
    delta_mixed = project_rest(parts, devices, me)
    attn_mixed = [project_rest(column_halves(total), devices, me) for total in done]
    return (delta_mixed, jnp.concatenate(attn_mixed, axis=0), final_state)


def solution(mesh):
    in_specs = (
        P("cache", None, "head"),
        P("cache", None, "head"),
        P("cache", None, "head"),
        P("cache", None, "head"),
        P("cache", "head", None),
        P("cache", "head", None),
        P("cache", "head", None, None),
        P("cache", "head", None, None),
        P("cache", "head", None, None),
        P("cache", None, "head"),
        P("cache", None, "head"),
        P(),
        P(),
        P("head", None),
        P("head", None),
    )
    out_specs = (
        P(("cache", "head"), None),
        P(("cache", "head"), None),
        P("cache", "head", None, None),
    )
    return jax.shard_map(
        on_device, mesh=mesh, in_specs=in_specs, out_specs=out_specs, check_vma=False
    )
```

```python
import functools
import math

import jax
import jax.numpy as jnp
from jax import lax
from jax.experimental import pallas as pl
from jax.experimental.pallas import tpu as pltpu
from jax.sharding import PartitionSpec as P

LK = 128
LV = 128
AH = 16
KVH = 2
HD = 256
BLOCK = 128
PAIR = 2
PARTS = 2
CHUNKS = 2

big_negative = -1e30
f32 = jnp.float32
bf16 = jnp.bfloat16


def mm(a, b, dims=((1,), (0,))):
    return lax.dot_general(a, b, (dims, ((), ())), preferred_element_type=f32)


def delta_kernel(deps, source, q_ref, k_ref, v_ref, gate_ref, row_ref, col_ref, start_ref, *refs):
    heads_ref, state_ref = refs[deps:]
    sessions, _, q_cols = q_ref.shape
    key_heads = q_cols // LK
    value_heads = v_ref.shape[2] // LV
    ratio = value_heads // key_heads

    @pl.when(pl.program_id(0) == 0)
    def _():
        for s in range(sessions):
            state_ref[s] = start_ref[source[s]].astype(f32)

    rows = lax.broadcasted_iota(jnp.int32, (BLOCK, BLOCK), 0)
    cols = lax.broadcasted_iota(jnp.int32, (BLOCK, BLOCK), 1)
    inclusive = rows >= cols
    differ = jnp.where(rows > cols, rows ^ cols, 0)
    eye = jnp.where(rows == cols, 1.0, 0.0).astype(f32)

    work = []
    for s in range(sessions):
        for a in range(key_heads):
            span = slice(a * LK, (a + 1) * LK)
            q = q_ref[s, :, span].astype(f32)
            k = k_ref[s, :, span].astype(f32)
            q = q * (lax.rsqrt(jnp.sum(q * q, axis=-1, keepdims=True) + 1e-06) * (1.0 / math.sqrt(LK)))
            k = k * lax.rsqrt(jnp.sum(k * k, axis=-1, keepdims=True) + 1e-06)
            qb, kb = q.astype(bf16), k.astype(bf16)
            key_key = mm(kb, kb, ((1,), (1,)))
            query_key = mm(qb, kb, ((1,), (1,)))
            for j in range(a * ratio, (a + 1) * ratio):
                run_row = row_ref[s, j : j + 1, :]
                run_col = col_ref[s, :, j : j + 1]
                strength = col_ref[s, :, value_heads + j : value_heads + j + 1]
                fall = jnp.where(inclusive, jnp.exp(jnp.minimum(run_col - run_row, 0.0)), 0.0)
                lower = strength * fall * key_key
                mixed = (fall * query_key).astype(bf16)
                growth = jnp.exp(run_col)
                v = v_ref[s, :, j * LV : (j + 1) * LV].astype(f32)
                right = jnp.concatenate([(strength * growth) * k, strength * v], axis=1).astype(bf16)
                last = run_row[:, BLOCK - 1 : BLOCK]
                tail = (jnp.exp(last - run_col) * k).astype(bf16)
                work.append((s, j, lower, mixed, (growth * q).astype(bf16), right, tail, jnp.exp(last)))

    inverses = [eye - jnp.where(differ == 1, item[2], 0.0) for item in work]
    for level in range(1, BLOCK.bit_length() - 1):
        mask = (differ >> level) == 1
        small = [t.astype(bf16) for t in inverses]
        first = [
            mm(jnp.where(mask, item[2], 0.0).astype(bf16), t).astype(bf16) for item, t in zip(work, small)
        ]
        inverses = [t - mm(b, x) for t, b, x in zip(inverses, small, first)]

    solved = [mm(t.astype(bf16), item[5]) for t, item in zip(inverses, work)]
    for item, x in zip(work, solved):
        s, j, _, mixed, q_grown, _, tail, fade = item
        state = state_ref[s, j]
        seen = mm(jnp.concatenate([x[:, :LK].astype(bf16), q_grown], axis=0), state.astype(bf16))
        update = (x[:, LK:] - seen[:BLOCK]).astype(bf16)
        state_ref[s, j] = fade * state + mm(tail, update, ((0,), (0,)))
        emitted = seen[BLOCK:] + mm(mixed, update)
        scale = lax.rsqrt(jnp.mean(emitted * emitted, axis=-1, keepdims=True) + 1e-06)
        gate = gate_ref[s, :, j * LV : (j + 1) * LV].astype(f32)
        heads_ref[s, :, j * LV : (j + 1) * LV] = (emitted * scale * (gate / (1.0 + jnp.exp(-gate)))).astype(bf16)


def block_rates(strength, decay):
    count, value_heads, fresh_len = decay.shape
    upto = jnp.triu(jnp.ones((BLOCK, BLOCK), f32))
    running = jnp.matmul(decay.reshape(-1, BLOCK), upto, precision=lax.Precision.HIGHEST)
    running = running.reshape(count, value_heads, fresh_len)
    return running, jnp.concatenate([running, strength], axis=1).transpose(0, 2, 1)


def delta_part(q, k, v, gate, running, columns, start, places, heads, pair, part, deps):
    count, fresh_len, value_cols = v.shape
    value_heads = value_cols // LV
    steps = fresh_len // BLOCK // PARTS
    unread = ([] if heads is None else [heads]) + list(deps)

    def rows(width):
        return pl.BlockSpec((PAIR, BLOCK, width), lambda c, _: (pair, part * steps + c, 0))

    return pl.pallas_call(
        functools.partial(delta_kernel, len(unread)),
        grid_spec=pltpu.PrefetchScalarGridSpec(
            num_scalar_prefetch=1,
            grid=(steps,),
            in_specs=[
                rows(q.shape[2]),
                rows(k.shape[2]),
                rows(value_cols),
                rows(value_cols),
                pl.BlockSpec((PAIR, value_heads, BLOCK), lambda c, _: (pair, 0, part * steps + c)),
                rows(2 * value_heads),
                pl.BlockSpec(start.shape, lambda c, _: (0, 0, 0, 0)),
            ]
            + [pl.BlockSpec(memory_space=pltpu.HBM)] * len(unread),
            out_specs=[
                rows(value_cols),
                pl.BlockSpec((PAIR, value_heads, LK, LV), lambda c, _: (0, 0, 0, 0)),
            ],
        ),
        out_shape=[
            jax.ShapeDtypeStruct((count, fresh_len, value_cols), bf16),
            jax.ShapeDtypeStruct((PAIR, value_heads, LK, LV), f32),
        ],
        input_output_aliases={} if heads is None else {8: 0},
        compiler_params=pltpu.CompilerParams(vmem_limit_bytes=60 * 2**20),
        cost_estimate=pl.CostEstimate(flops=10**10, bytes_accessed=3 * 10**6, transcendentals=0),
        name="delta_part",
    )(places, q, k, v, gate, running, columns, start, *unread)


def attend_kernel(chunk, block_rows, devices, scalars, lengths, q_ref, gate_ref, near_ref, far_ref, fresh_ref, *refs):
    out_ref = refs[-1]
    s = pl.program_id(0)
    me = scalars[1]
    length = lengths[s]
    _, blocks, part, width = q_ref.shape
    rows = blocks * part
    heads = width // HD
    slots, _, _, kept_rows, _ = near_ref.shape
    kept = slots * kept_rows
    bits = devices.bit_length() - 1

    def penalty(far):
        lane = lax.broadcasted_iota(jnp.int32, (1, kept), 1)
        slot = lane // kept_rows + far * slots
        code = jnp.zeros_like(slot)
        for i in range(bits):
            code = code + ((slot >> i) & 1) * (1 << (bits - 1 - i))
        place = (code ^ me) * kept_rows + lane % kept_rows
        return jnp.where(place < length, 0.0, big_negative).astype(f32)

    fresh = fresh_ref.shape[0] * fresh_ref.shape[3]
    row = lax.broadcasted_iota(jnp.int32, (rows, fresh), 0)
    now = (row // part) * block_rows + chunk * part + row % part
    causal = lax.broadcasted_iota(jnp.int32, (rows, fresh), 1) <= now
    near_off, far_off = penalty(0), penalty(1)

    keys = [
        near_ref[:, 0, 0].reshape(kept, HD),
        far_ref[:, 0, 0].reshape(kept, HD),
        fresh_ref[:, 0, 0].reshape(fresh, HD),
    ]
    values = [
        near_ref[:, 0, 1].reshape(kept, HD),
        far_ref[:, 0, 1].reshape(kept, HD),
        fresh_ref[:, 1, 0].reshape(fresh, HD),
    ]
    for h in range(heads):
        q = q_ref[0, :, :, h * HD : (h + 1) * HD].reshape(rows, HD)
        near = mm(q, keys[0], ((1,), (1,))) + near_off
        far = mm(q, keys[1], ((1,), (1,))) + far_off
        new = jnp.where(causal, mm(q, keys[2], ((1,), (1,))), big_negative)
        peak = jnp.max(jnp.maximum(jnp.maximum(near, far), new) if kept == fresh else new, axis=-1, keepdims=True)
        if kept != fresh:
            peak = jnp.maximum(peak, jnp.max(jnp.maximum(near, far), axis=-1, keepdims=True))
        weights = [jnp.exp((x - peak) * (1.0 / math.sqrt(HD))) for x in (near, far, new)]
        total = sum(jnp.sum(w, axis=-1, keepdims=True) for w in weights)
        mixed = sum(mm(w.astype(bf16), v) for w, v in zip(weights, values))
        gate = gate_ref[0, :, :, h * HD : (h + 1) * HD].reshape(rows, HD).astype(f32)
        gated = mixed / (total * (1.0 + jnp.exp(-gate)))
        out_ref[0, :, :, h * HD : (h + 1) * HD] = gated.astype(bf16).reshape(blocks, part, HD)


def attend(chunk, block_rows, devices, q, gate, near, far, fresh, scalars, lengths, places, deps):
    count, blocks, _, width = q.shape
    part = block_rows // CHUNKS
    scalars = jnp.concatenate([scalars, places])
    slots, _, _, kept_rows, _ = near.shape
    rows = pl.BlockSpec((1, blocks, part, width), lambda s, m, n: (s, 0, chunk, 0))
    kept = pl.BlockSpec((slots, 1, 2, kept_rows, HD), lambda s, m, n: (0, m[2 + s], 0, 0, 0))
    return pl.pallas_call(
        functools.partial(attend_kernel, chunk, block_rows, devices),
        grid_spec=pltpu.PrefetchScalarGridSpec(
            num_scalar_prefetch=2,
            grid=(count,),
            in_specs=[
                rows,
                rows,
                kept,
                kept,
                pl.BlockSpec(
                    (fresh.shape[0], 2, 1, fresh.shape[3], HD), lambda s, m, n: (0, 0, s, 0, m[0])
                ),
            ]
            + [pl.BlockSpec(memory_space=pl.ANY)] * len(deps),
            out_specs=pl.BlockSpec((1, blocks, part, width), lambda s, m, n: (s, 0, 0, 0)),
        ),
        out_shape=jax.ShapeDtypeStruct((count, blocks, part, width), bf16),
        compiler_params=pltpu.CompilerParams(vmem_limit_bytes=48 * 2**20),
        cost_estimate=pl.CostEstimate(flops=10**10, bytes_accessed=8 * 10**6, transcendentals=0),
        name="attend",
    )(scalars, lengths, q, gate, near, far, fresh, *deps)


def swap(x, devices, bit, axis="head"):
    return lax.ppermute(x, axis, [(h, h ^ bit) for h in range(devices)])


def halves(x, me, bit, lowest):
    split = x.reshape(x.shape[0] // (2 * lowest), 2, lowest, *x.shape[1:])
    mine = (me // bit) % 2

    def pick(which):
        got = lax.dynamic_index_in_dim(split, which, 1, keepdims=False)
        return got.reshape(x.shape[0] // 2, *x.shape[1:])

    return pick(mine), pick(1 - mine)


def add(a, b):
    return (a.astype(f32) + b.astype(f32)).astype(bf16)


def product(x, weight):
    out = jnp.dot(x.reshape(-1, x.shape[2]), weight, preferred_element_type=f32)
    return out.astype(bf16).reshape(x.shape[0], x.shape[1], -1)


def project_first(heads, weight, devices, me):
    kept, sent = halves(heads, me, 1, 1)
    outgoing = product(sent, weight)
    return outgoing, add(product(kept, weight), swap(outgoing, devices, 1))


def project_next(parts, devices, me):
    bits = devices.bit_length() - 1
    orders = (list(range(1, bits)), list(range(bits - 1, 0, -1)))
    done = []
    for part, order in zip(parts, orders):
        left = part.shape[0].bit_length() - 1
        bit = order[bits - 1 - left]
        below = sum(1 for b in order[bits - 1 - left :] if b < bit)
        mine, other = halves(part, me, 1 << bit, 1 << below)
        done.append(add(mine, swap(other, devices, 1 << bit)))
    return done


def column_halves(total):
    wide = total.shape[2] // 2
    return [total[:, :, :wide], total[:, :, wide:]]


def project_rest(parts, devices, me):
    while parts[0].shape[0] > 1:
        parts = project_next(parts, devices, me)
    return jnp.concatenate([p[0] for p in parts], axis=1)


def on_device(
    delta_query,
    delta_key,
    delta_value,
    delta_gate,
    write_strength,
    decay_log,
    kept_state,
    kept_kv,
    fresh_kv,
    attn_query,
    attn_gate,
    cached_len,
    slot_of_session,
    delta_out_weight,
    attn_out_weight,
):
    count, fresh_len, query_cols = attn_query.shape
    owners = lax.axis_size("cache")
    devices = lax.axis_size("head")
    owner_id = lax.axis_index("cache")
    me = lax.axis_index("head")
    session_ids = jnp.arange(slot_of_session.shape[0], dtype=jnp.int32)
    on_mine = slot_of_session // count == owner_id
    owner_of = session_ids // count
    wanted = on_mine[None, :] & (owner_of[None, :] == jnp.arange(owners, dtype=jnp.int32)[:, None])
    picked_slot = jnp.sum(jnp.where(wanted, slot_of_session[None, :] - owner_id * count, 0), axis=1)
    my_slots = lax.dynamic_slice_in_dim(slot_of_session, owner_id * count, count)
    source = my_slots // count
    lengths = lax.dynamic_slice_in_dim(cached_len, owner_id * count, count)

    places = source ^ owner_id

    def send_on(x, distance):
        block = lax.dynamic_slice_in_dim(x, picked_slot[owner_id ^ distance], 1, 0)
        return swap(block, owners, distance, "cache") if distance else block

    state_bf16 = kept_state.astype(bf16)
    start = jnp.concatenate([send_on(state_bf16, r) for r in range(owners)], axis=0)

    heads_dev = query_cols // HD
    kv_head = me * heads_dev // (AH // KVH)
    fresh_all = lax.all_gather(fresh_kv.transpose(2, 0, 1, 3), "head", axis=0, tiled=False)

    half = devices // 2
    own = lax.dynamic_slice_in_dim(kept_kv, kv_head * HD, HD, 3).transpose(0, 2, 1, 3)
    other = lax.dynamic_slice_in_dim(kept_kv, (1 - kv_head) * HD, HD, 3).transpose(0, 2, 1, 3)
    both = jnp.stack([own, swap(other, devices, half)], axis=1)
    blocks = [send_on(both, r) for r in range(owners)]

    calls = count // PAIR * PARTS
    bit = half // 2
    crossed = [swap(block, devices, bit) for block in blocks]
    needed = [[] for _ in range(calls - 1)]
    for r in range(1, owners):
        arrival = min((r - 1) * (calls - 1) // (owners - 1), calls - 2)
        needed[arrival].append(blocks[r])
        if arrival + 1 < calls - 1:
            needed[arrival + 1].append(crossed[r])
    needed[min(1, calls - 2)].append(crossed[0])
    needed[-1].append(fresh_all)

    running, columns = block_rates(write_strength, decay_log)
    heads, states, call = None, [], 0
    for pair in range(count // PAIR):
        begin, index = start, lax.slice_in_dim(places, pair * PAIR, (pair + 1) * PAIR)
        for part in range(PARTS):
            deps = needed[call - 1] if call else []
            heads, begin = delta_part(
                delta_query,
                delta_key,
                delta_value,
                delta_gate,
                running,
                columns,
                begin,
                index,
                heads,
                pair,
                part,
                deps,
            )
            index = jnp.arange(PAIR, dtype=jnp.int32)
            call += 1
        states.append(begin)
    final_state = jnp.concatenate(states, axis=0)

    near = [jnp.stack([x[0] for x in side], axis=1) for side in (blocks, crossed)]
    near = jnp.concatenate(near, axis=0)
    bit //= 2
    while bit > 1:
        near = jnp.concatenate([near, swap(near, devices, bit)], axis=0)
        bit //= 2
    far = swap(near, devices, 1)

    block_rows = count * fresh_len // devices
    _, total = project_first(heads.reshape(devices, block_rows, -1), delta_out_weight, devices, me)
    scalars = jnp.stack([kv_head, me]).astype(jnp.int32)
    q4 = attn_query.reshape(count, fresh_len // block_rows, block_rows, query_cols)
    gate4 = attn_gate.reshape(q4.shape)
    parts = column_halves(total)
    deps = [total]
    done = []
    for chunk in range(CHUNKS):
        mixed = attend(
            chunk, block_rows, devices, q4, gate4, near, far, fresh_all, scalars, lengths, places, deps
        )
        mixed = mixed.reshape(devices, block_rows // CHUNKS, query_cols)
        outgoing, total = project_first(mixed, attn_out_weight, devices, me)
        if parts[0].shape[0] > 1:
            parts = project_next(parts, devices, me)
        deps = [outgoing, *parts]
        done.append(total)
    delta_mixed = project_rest(parts, devices, me)
    attn_mixed = [project_rest(column_halves(total), devices, me) for total in done]
    return (delta_mixed, jnp.concatenate(attn_mixed, axis=0), final_state)


def solution(mesh):
    in_specs = (
        P("cache", None, "head"),
        P("cache", None, "head"),
        P("cache", None, "head"),
        P("cache", None, "head"),
        P("cache", "head", None),
        P("cache", "head", None),
        P("cache", "head", None, None),
        P("cache", "head", None, None),
        P("cache", "head", None, None),
        P("cache", None, "head"),
        P("cache", None, "head"),
        P(),
        P(),
        P("head", None),
        P("head", None),
    )
    out_specs = (
        P(("cache", "head"), None),
        P(("cache", "head"), None),
        P("cache", "head", None, None),
    )
    return jax.shard_map(
        on_device, mesh=mesh, in_specs=in_specs, out_specs=out_specs, check_vma=False
    )
```

```python
import functools
import math

import jax
import jax.numpy as jnp
from jax import lax
from jax.experimental import pallas as pl
from jax.experimental.pallas import tpu as pltpu
from jax.sharding import PartitionSpec as P

LK = 128
LV = 128
AH = 16
KVH = 2
HD = 256
BLOCK = 128
PAIR = 2
PARTS = 2
CHUNKS = 2

big_negative = -1e30
f32 = jnp.float32
bf16 = jnp.bfloat16


def mm(a, b, dims=((1,), (0,))):
    return lax.dot_general(a, b, (dims, ((), ())), preferred_element_type=f32)


def delta_kernel(deps, source, q_ref, k_ref, v_ref, gate_ref, row_ref, col_ref, start_ref, *refs):
    heads_ref, state_ref = refs[deps:]
    sessions, _, q_cols = q_ref.shape
    key_heads = q_cols // LK
    value_heads = v_ref.shape[2] // LV
    ratio = value_heads // key_heads

    @pl.when(pl.program_id(0) == 0)
    def _():
        for s in range(sessions):
            state_ref[s] = start_ref[source[s]].astype(f32)

    rows = lax.broadcasted_iota(jnp.int32, (BLOCK, BLOCK), 0)
    cols = lax.broadcasted_iota(jnp.int32, (BLOCK, BLOCK), 1)
    inclusive = rows >= cols
    differ = jnp.where(rows > cols, rows ^ cols, 0)
    eye = jnp.where(rows == cols, 1.0, 0.0).astype(f32)

    work = []
    for s in range(sessions):
        for a in range(key_heads):
            span = slice(a * LK, (a + 1) * LK)
            q = q_ref[s, :, span].astype(f32)
            k = k_ref[s, :, span].astype(f32)
            q = q * (lax.rsqrt(jnp.sum(q * q, axis=-1, keepdims=True) + 1e-06) * (1.0 / math.sqrt(LK)))
            k = k * lax.rsqrt(jnp.sum(k * k, axis=-1, keepdims=True) + 1e-06)
            qb, kb = q.astype(bf16), k.astype(bf16)
            key_key = mm(kb, kb, ((1,), (1,)))
            query_key = mm(qb, kb, ((1,), (1,)))
            for j in range(a * ratio, (a + 1) * ratio):
                run_row = row_ref[s, j : j + 1, :]
                run_col = col_ref[s, :, j : j + 1]
                strength = col_ref[s, :, value_heads + j : value_heads + j + 1]
                fall = jnp.where(inclusive, jnp.exp(jnp.minimum(run_col - run_row, 0.0)), 0.0)
                lower = strength * fall * key_key
                mixed = (fall * query_key).astype(bf16)
                growth = jnp.exp(run_col)
                v = v_ref[s, :, j * LV : (j + 1) * LV].astype(f32)
                right = jnp.concatenate([(strength * growth) * k, strength * v], axis=1).astype(bf16)
                last = run_row[:, BLOCK - 1 : BLOCK]
                tail = (jnp.exp(last - run_col) * k).astype(bf16)
                work.append((s, j, lower, mixed, (growth * q).astype(bf16), right, tail, jnp.exp(last)))

    inverses = [eye - jnp.where(differ == 1, item[2], 0.0) for item in work]
    for level in range(1, BLOCK.bit_length() - 1):
        mask = (differ >> level) == 1
        small = [t.astype(bf16) for t in inverses]
        first = [
            mm(jnp.where(mask, item[2], 0.0).astype(bf16), t).astype(bf16) for item, t in zip(work, small)
        ]
        inverses = [t - mm(b, x) for t, b, x in zip(inverses, small, first)]

    solved = [mm(t.astype(bf16), item[5]) for t, item in zip(inverses, work)]
    for item, x in zip(work, solved):
        s, j, _, mixed, q_grown, _, tail, fade = item
        state = state_ref[s, j]
        seen = mm(jnp.concatenate([x[:, :LK].astype(bf16), q_grown], axis=0), state.astype(bf16))
        update = (x[:, LK:] - seen[:BLOCK]).astype(bf16)
        state_ref[s, j] = fade * state + mm(tail, update, ((0,), (0,)))
        emitted = seen[BLOCK:] + mm(mixed, update)
        scale = lax.rsqrt(jnp.mean(emitted * emitted, axis=-1, keepdims=True) + 1e-06)
        gate = gate_ref[s, :, j * LV : (j + 1) * LV].astype(f32)
        heads_ref[s, :, j * LV : (j + 1) * LV] = (emitted * scale * (gate / (1.0 + jnp.exp(-gate)))).astype(bf16)


def block_rates(strength, decay):
    count, value_heads, fresh_len = decay.shape
    upto = jnp.triu(jnp.ones((BLOCK, BLOCK), f32))
    running = jnp.matmul(decay.reshape(-1, BLOCK), upto, precision=lax.Precision.HIGHEST)
    running = running.reshape(count, value_heads, fresh_len)
    return running, jnp.concatenate([running, strength], axis=1).transpose(0, 2, 1)


def delta_part(q, k, v, gate, running, columns, start, places, heads, pair, part, deps):
    count, fresh_len, value_cols = v.shape
    value_heads = value_cols // LV
    steps = fresh_len // BLOCK // PARTS
    unread = ([] if heads is None else [heads]) + list(deps)

    def rows(width):
        return pl.BlockSpec((PAIR, BLOCK, width), lambda c, _: (pair, part * steps + c, 0))

    return pl.pallas_call(
        functools.partial(delta_kernel, len(unread)),
        grid_spec=pltpu.PrefetchScalarGridSpec(
            num_scalar_prefetch=1,
            grid=(steps,),
            in_specs=[
                rows(q.shape[2]),
                rows(k.shape[2]),
                rows(value_cols),
                rows(value_cols),
                pl.BlockSpec((PAIR, value_heads, BLOCK), lambda c, _: (pair, 0, part * steps + c)),
                rows(2 * value_heads),
                pl.BlockSpec(start.shape, lambda c, _: (0, 0, 0, 0)),
            ]
            + [pl.BlockSpec(memory_space=pltpu.HBM)] * len(unread),
            out_specs=[
                rows(value_cols),
                pl.BlockSpec((PAIR, value_heads, LK, LV), lambda c, _: (0, 0, 0, 0)),
            ],
        ),
        out_shape=[
            jax.ShapeDtypeStruct((count, fresh_len, value_cols), bf16),
            jax.ShapeDtypeStruct((PAIR, value_heads, LK, LV), f32),
        ],
        input_output_aliases={} if heads is None else {8: 0},
        compiler_params=pltpu.CompilerParams(vmem_limit_bytes=60 * 2**20),
        cost_estimate=pl.CostEstimate(flops=10**10, bytes_accessed=3 * 10**6, transcendentals=0),
        name="delta_part",
    )(places, q, k, v, gate, running, columns, start, *unread)


def attend_kernel(chunk, block_rows, devices, scalars, lengths, q_ref, gate_ref, near_ref, far_ref, fresh_ref, *refs):
    out_ref = refs[-1]
    s = pl.program_id(0)
    me = scalars[1]
    length = lengths[s]
    _, blocks, part, width = q_ref.shape
    rows = blocks * part
    heads = width // HD
    slots, _, _, kept_rows, _ = near_ref.shape
    kept = slots * kept_rows
    bits = devices.bit_length() - 1

    def penalty(far):
        lane = lax.broadcasted_iota(jnp.int32, (1, kept), 1)
        slot = lane // kept_rows + far * slots
        code = jnp.zeros_like(slot)
        for i in range(bits):
            code = code + ((slot >> i) & 1) * (1 << (bits - 1 - i))
        place = (code ^ me) * kept_rows + lane % kept_rows
        return jnp.where(place < length, 0.0, big_negative).astype(f32)

    fresh = fresh_ref.shape[0] * fresh_ref.shape[3]
    row = lax.broadcasted_iota(jnp.int32, (rows, fresh), 0)
    now = (row // part) * block_rows + chunk * part + row % part
    causal = lax.broadcasted_iota(jnp.int32, (rows, fresh), 1) <= now
    near_off, far_off = penalty(0), penalty(1)

    keys = [
        near_ref[:, 0, 0].reshape(kept, HD),
        far_ref[:, 0, 0].reshape(kept, HD),
        fresh_ref[:, 0, 0].reshape(fresh, HD),
    ]
    values = [
        near_ref[:, 0, 1].reshape(kept, HD),
        far_ref[:, 0, 1].reshape(kept, HD),
        fresh_ref[:, 1, 0].reshape(fresh, HD),
    ]
    for h in range(heads):
        q = q_ref[0, :, :, h * HD : (h + 1) * HD].reshape(rows, HD)
        near = mm(q, keys[0], ((1,), (1,))) + near_off
        far = mm(q, keys[1], ((1,), (1,))) + far_off
        new = jnp.where(causal, mm(q, keys[2], ((1,), (1,))), big_negative)
        peak = jnp.max(jnp.maximum(jnp.maximum(near, far), new) if kept == fresh else new, axis=-1, keepdims=True)
        if kept != fresh:
            peak = jnp.maximum(peak, jnp.max(jnp.maximum(near, far), axis=-1, keepdims=True))
        weights = [jnp.exp((x - peak) * (1.0 / math.sqrt(HD))) for x in (near, far, new)]
        total = sum(jnp.sum(w, axis=-1, keepdims=True) for w in weights)
        mixed = sum(mm(w.astype(bf16), v) for w, v in zip(weights, values))
        gate = gate_ref[0, :, :, h * HD : (h + 1) * HD].reshape(rows, HD).astype(f32)
        gated = mixed / (total * (1.0 + jnp.exp(-gate)))
        out_ref[0, :, :, h * HD : (h + 1) * HD] = gated.astype(bf16).reshape(blocks, part, HD)


def attend(chunk, block_rows, devices, q, gate, near, far, fresh, scalars, lengths, places, deps):
    count, blocks, _, width = q.shape
    part = block_rows // CHUNKS
    scalars = jnp.concatenate([scalars, places])
    slots, _, _, kept_rows, _ = near.shape
    rows = pl.BlockSpec((1, blocks, part, width), lambda s, m, n: (s, 0, chunk, 0))
    kept = pl.BlockSpec((slots, 1, 2, kept_rows, HD), lambda s, m, n: (0, m[2 + s], 0, 0, 0))
    return pl.pallas_call(
        functools.partial(attend_kernel, chunk, block_rows, devices),
        grid_spec=pltpu.PrefetchScalarGridSpec(
            num_scalar_prefetch=2,
            grid=(count,),
            in_specs=[
                rows,
                rows,
                kept,
                kept,
                pl.BlockSpec(
                    (fresh.shape[0], 2, 1, fresh.shape[3], HD), lambda s, m, n: (0, 0, s, 0, m[0])
                ),
            ]
            + [pl.BlockSpec(memory_space=pl.ANY)] * len(deps),
            out_specs=pl.BlockSpec((1, blocks, part, width), lambda s, m, n: (s, 0, 0, 0)),
        ),
        out_shape=jax.ShapeDtypeStruct((count, blocks, part, width), bf16),
        compiler_params=pltpu.CompilerParams(vmem_limit_bytes=48 * 2**20),
        cost_estimate=pl.CostEstimate(flops=10**10, bytes_accessed=8 * 10**6, transcendentals=0),
        name="attend",
    )(scalars, lengths, q, gate, near, far, fresh, *deps)


def swap(x, devices, bit, axis="head"):
    return lax.ppermute(x, axis, [(h, h ^ bit) for h in range(devices)])


def halves(x, me, bit, lowest):
    split = x.reshape(x.shape[0] // (2 * lowest), 2, lowest, *x.shape[1:])
    mine = (me // bit) % 2

    def pick(which):
        got = lax.dynamic_index_in_dim(split, which, 1, keepdims=False)
        return got.reshape(x.shape[0] // 2, *x.shape[1:])

    return pick(mine), pick(1 - mine)


def add(a, b):
    return (a.astype(f32) + b.astype(f32)).astype(bf16)


def product(x, weight):
    out = jnp.dot(x.reshape(-1, x.shape[2]), weight, preferred_element_type=f32)
    return out.astype(bf16).reshape(x.shape[0], x.shape[1], -1)


def project_first(heads, weight, devices, me):
    kept, sent = halves(heads, me, 1, 1)
    outgoing = product(sent, weight)
    return outgoing, add(product(kept, weight), swap(outgoing, devices, 1))


def project_next(parts, devices, me):
    bits = devices.bit_length() - 1
    orders = (list(range(1, bits)), list(range(bits - 1, 0, -1)))
    done = []
    for part, order in zip(parts, orders):
        left = part.shape[0].bit_length() - 1
        bit = order[bits - 1 - left]
        below = sum(1 for b in order[bits - 1 - left :] if b < bit)
        mine, other = halves(part, me, 1 << bit, 1 << below)
        done.append(add(mine, swap(other, devices, 1 << bit)))
    return done


def column_halves(total):
    wide = total.shape[2] // 2
    return [total[:, :, :wide], total[:, :, wide:]]


def project_rest(parts, devices, me):
    while parts[0].shape[0] > 1:
        parts = project_next(parts, devices, me)
    return jnp.concatenate([p[0] for p in parts], axis=1)


def on_device(
    delta_query,
    delta_key,
    delta_value,
    delta_gate,
    write_strength,
    decay_log,
    kept_state,
    kept_kv,
    fresh_kv,
    attn_query,
    attn_gate,
    cached_len,
    slot_of_session,
    delta_out_weight,
    attn_out_weight,
):
    count, fresh_len, query_cols = attn_query.shape
    owners = lax.axis_size("cache")
    devices = lax.axis_size("head")
    owner_id = lax.axis_index("cache")
    me = lax.axis_index("head")
    session_ids = jnp.arange(slot_of_session.shape[0], dtype=jnp.int32)
    on_mine = slot_of_session // count == owner_id
    owner_of = session_ids // count
    wanted = on_mine[None, :] & (owner_of[None, :] == jnp.arange(owners, dtype=jnp.int32)[:, None])
    picked_slot = jnp.sum(jnp.where(wanted, slot_of_session[None, :] - owner_id * count, 0), axis=1)
    my_slots = lax.dynamic_slice_in_dim(slot_of_session, owner_id * count, count)
    source = my_slots // count
    lengths = lax.dynamic_slice_in_dim(cached_len, owner_id * count, count)

    places = source ^ owner_id

    def send_on(x, distance):
        block = lax.dynamic_slice_in_dim(x, picked_slot[owner_id ^ distance], 1, 0)
        return swap(block, owners, distance, "cache") if distance else block

    state_bf16 = kept_state.astype(bf16)
    start = jnp.concatenate([send_on(state_bf16, r) for r in range(owners)], axis=0)

    heads_dev = query_cols // HD
    kv_head = me * heads_dev // (AH // KVH)
    fresh_all = lax.all_gather(fresh_kv.transpose(2, 0, 1, 3), "head", axis=0, tiled=False)

    half = devices // 2
    own = lax.dynamic_slice_in_dim(kept_kv, kv_head * HD, HD, 3).transpose(0, 2, 1, 3)
    other = lax.dynamic_slice_in_dim(kept_kv, (1 - kv_head) * HD, HD, 3).transpose(0, 2, 1, 3)
    both = jnp.stack([own, swap(other, devices, half)], axis=1)
    blocks = [send_on(both, r) for r in range(owners)]

    calls = count // PAIR * PARTS
    bit = half // 2
    crossed = [swap(block, devices, bit) for block in blocks]
    needed = [[] for _ in range(calls - 1)]
    for r in range(1, owners):
        arrival = min((r - 1) * (calls - 1) // (owners - 1) + 1, calls - 2)
        needed[arrival].append(blocks[r])
        if arrival + 1 < calls - 1:
            needed[arrival + 1].append(crossed[r])
    needed[min(1, calls - 2)].append(crossed[0])
    needed[-1].append(fresh_all)

    running, columns = block_rates(write_strength, decay_log)
    heads, states, call = None, [], 0
    for pair in range(count // PAIR):
        begin, index = start, lax.slice_in_dim(places, pair * PAIR, (pair + 1) * PAIR)
        for part in range(PARTS):
            deps = needed[call - 1] if call else []
            heads, begin = delta_part(
                delta_query,
                delta_key,
                delta_value,
                delta_gate,
                running,
                columns,
                begin,
                index,
                heads,
                pair,
                part,
                deps,
            )
            index = jnp.arange(PAIR, dtype=jnp.int32)
            call += 1
        states.append(begin)
    final_state = jnp.concatenate(states, axis=0)

    near = [jnp.stack([x[0] for x in side], axis=1) for side in (blocks, crossed)]
    near = jnp.concatenate(near, axis=0)
    bit //= 2
    while bit > 1:
        near = jnp.concatenate([near, swap(near, devices, bit)], axis=0)
        bit //= 2
    far = swap(near, devices, 1)

    block_rows = count * fresh_len // devices
    _, total = project_first(heads.reshape(devices, block_rows, -1), delta_out_weight, devices, me)
    scalars = jnp.stack([kv_head, me]).astype(jnp.int32)
    q4 = attn_query.reshape(count, fresh_len // block_rows, block_rows, query_cols)
    gate4 = attn_gate.reshape(q4.shape)
    parts = column_halves(total)
    deps = [total]
    done = []
    for chunk in range(CHUNKS):
        mixed = attend(
            chunk, block_rows, devices, q4, gate4, near, far, fresh_all, scalars, lengths, places, deps
        )
        mixed = mixed.reshape(devices, block_rows // CHUNKS, query_cols)
        outgoing, total = project_first(mixed, attn_out_weight, devices, me)
        if parts[0].shape[0] > 1:
            parts = project_next(parts, devices, me)
        deps = [outgoing, *parts]
        done.append(total)
    delta_mixed = project_rest(parts, devices, me)
    attn_mixed = [project_rest(column_halves(total), devices, me) for total in done]
    return (delta_mixed, jnp.concatenate(attn_mixed, axis=0), final_state)


def solution(mesh):
    in_specs = (
        P("cache", None, "head"),
        P("cache", None, "head"),
        P("cache", None, "head"),
        P("cache", None, "head"),
        P("cache", "head", None),
        P("cache", "head", None),
        P("cache", "head", None, None),
        P("cache", "head", None, None),
        P("cache", "head", None, None),
        P("cache", None, "head"),
        P("cache", None, "head"),
        P(),
        P(),
        P("head", None),
        P("head", None),
    )
    out_specs = (
        P(("cache", "head"), None),
        P(("cache", "head"), None),
        P("cache", "head", None, None),
    )
    return jax.shard_map(
        on_device, mesh=mesh, in_specs=in_specs, out_specs=out_specs, check_vma=False
    )
```
